256 devices in a mesh: cp: 4 (over x_lo, core), tp: 4 (over y), dp: 16 (over z, x_hi).
Axes of the slice: x: 4 (x_hi: 2, x_lo: 2; x = x_hi * 2 + x_lo), y: 4, z: 8, core: 2. Of those that a mesh axis runs over, the one named last changes fastest.
Arguments:
- tokens: bfloat16 [32768, 4096], P(('dp', 'cp', 'tp')), parts along dimension 0, may hold values from -6 to 6
- cotangent: bfloat16 [32768, 4096], P(('dp', 'cp', 'tp')), parts along dimension 0, may hold values from -6 to 6
- routes: int32 [32768, 1], P(('dp', 'cp', 'tp')), parts along dimension 0, may hold values from 0 to 3; in each aligned block of 128 rows (0 to 127, 128 to 255, ...) at most 48 rows name the same one
- gate_fixed: int32 [32768], P(('dp', 'cp', 'tp')), parts along dimension 0, may hold values from 4096 to 65535
- w_gate: bfloat16 [4, 768, 4096], P('cp', 'tp'), may hold values from -0.09375 to 0.09375
- w_up: bfloat16 [4, 768, 4096], P('cp', 'tp'), may hold values from -0.09375 to 0.09375
- w_down: bfloat16 [4, 768, 4096], P('cp', 'tp'), may hold values from -0.21875 to 0.21875
Outputs:
- grad_tokens: bfloat16 [32768, 4096], P(('dp', 'cp', 'tp')), parts along dimension 0
- grad_gate: bfloat16 [64, 768, 4096], P(('dp', 'cp'), 'tp'), parts along dimension 0
- grad_up: bfloat16 [64, 768, 4096], P(('dp', 'cp'), 'tp'), parts along dimension 0
- grad_down: bfloat16 [64, 768, 4096], P(('dp', 'cp'), 'tp'), parts along dimension 0
The draws below stay inside these ranges and needn't reach their ends.
There are 16 independent parts, one for each index of `dp`. The reference program is written for one: setup_inputs(seed, part) draws one part's arguments, and reference() takes and returns one part's arrays. A program takes and returns all parts, laid end to end along the dimension named above; an argument that names none is the same for every part. Nothing has to cross between parts.
Inputs may be any that keep to these rules, and one draw needn't show every extreme that they name: `routes`: among the rows of one device no expert is named more than 48 times, a bound that some block reaches. `gate_fixed`: the router weight is the value divided by 65536.
All inputs are finite; a program needn't handle non-finite values.
Results may differ from the reference program's by a relative error of at most 0.0058.
Values may be sent and summed in bfloat16 or wider, within the bound.
No kernel may reach another device: no remote copies, remote signals or barrier semaphores. Data moves between devices by JAX's collectives and lax.ppermute only.
A program may use at most 128 MiB of HBM per device.

```python
import math
import jax
import jax.numpy as jnp
import numpy as np
from jax import lax

D = 4096
FF = 768
TOK_DEV = 128
TOKENS = 2048
EXPERTS = 4
CAP = 48
N_CP = 4
N_TP = 4


def place_ends(result, stream_key, least, largest):
    shape = result.shape
    place = [jax.random.randint(jax.random.fold_in(stream_key, axis), (), 0, shape[axis]) for axis in range(len(shape))]
    result = result.at[tuple(place)].set(least)
    longest = shape.index(max(shape))
    place[longest] = (place[longest] + 1) % shape[longest]
    return result.at[tuple(place)].set(largest)


def levels(rng, dims, split, smallest, high):
    def one(position, shards_of):
        draws = jax.random.uniform(jax.random.fold_in(jax.random.fold_in(rng, 6), position), (shards_of,), jnp.float32, smallest / len(split), high / len(split))
        return jnp.repeat(jnp.exp(draws), dims[position] // shards_of).reshape((-1,) + (1,) * (len(dims) - position - 1))

    factor_of = one(*split[0])
    for cut in split[1:]:
        factor_of = factor_of * one(*cut)
    return factor_of


def deal_out(own_key, own, number, rows, amount, top, limit, skew):
    order = jax.random.permutation(own_key, amount)
    heavy_load, usual = shares(amount, rows * top, limit, skew, True), shares(amount, rows * top, limit, skew, False)
    places = jnp.arange(amount)

    def named(sizes, offset_by):
        used = int((sizes > 0).sum())
        fixed = max(1, used // 4)
        passed = fixed + (places - fixed + offset_by * (used - fixed)) % max(1, amount - fixed)
        return jnp.zeros((amount,), jnp.int32).at[order[jnp.where(places < fixed, places, passed)]].set(jnp.asarray(sizes, jnp.int32))

    sizes = jnp.where(number % 4 == 0, named(heavy_load, number // 4), named(usual, number - number // 4 - 1))
    mixed = jax.random.permutation(jax.random.fold_in(own, 3), amount)
    source_of, receiver = mixed[0:amount // 2 * 2:2], mixed[1:amount // 2 * 2:2]
    slack = jnp.minimum(sizes[source_of] - 1, limit - sizes[receiver]) // 2
    slack = jnp.where((source_of == order[0]) | (receiver == order[0]) | (sizes[receiver] == 0), 0, jnp.maximum(slack, 0))
    passed = jax.random.randint(jax.random.fold_in(own, 4), (amount // 2,), 0, 1 << 20) % (slack + 1)
    sizes = sizes.at[source_of].add(-passed).at[receiver].add(passed)
    members = jnp.searchsorted(jnp.cumsum(sizes), jnp.arange(rows * top), side="right").astype(jnp.int32)
    grid = members.reshape(top, rows).T
    grid = grid[jax.random.permutation(jax.random.fold_in(own, 1), rows)]
    offset_by = jax.random.randint(jax.random.fold_in(own, 2), (rows, 1), 0, top)
    return jnp.take_along_axis(grid, (jnp.arange(top)[None, :] + offset_by) % top, axis=1)


def shares(number_of, total, bound, skew, full):
    weights = [(1 << 20) // math.isqrt(grade ** skew) + 1 for grade in range(1, number_of + 1)]
    largest = bound if full else min(bound, max(-(-total // number_of), total * weights[0] // sum(weights)))
    least = 1 if total - largest >= number_of - 1 else 0
    given, surplus = [largest] + [least] * (number_of - 1), total - largest - least * (number_of - 1)
    while surplus > 0:
        movable = [i for i in range(1, number_of) if given[i] < largest] or [i for i in range(1, number_of) if given[i] < bound]
        mass, left = sum([weights[i] for i in movable]), surplus
        for i in movable:
            more = min(bound - given[i], max(1, left * weights[i] // mass), surplus)
            given[i] = given[i] + more
            surplus = surplus - more
    return np.array(given)


def centred(stream_key, extent, deviation, limit, pieces=(), dtype=jnp.bfloat16):
    drawn = deviation * jax.random.normal(stream_key, extent, jnp.float32)
    if pieces:
        drawn = drawn * levels(stream_key, extent, pieces, -0.22, 0.18)
    return jnp.clip(drawn, -limit, limit).astype(dtype)


def setup_inputs(seed: int = 0, part: int = 0) -> dict:
    seeds = jax.random.split(jax.random.key(seed), 8)
    own_keys = jax.random.split(jax.random.fold_in(seeds[7], part), 8)
    tokens = centred(own_keys[0], (TOKENS, D), 1.0, 6.0, ((0, 16),))
    cotangent = centred(own_keys[1], (TOKENS, D), 1.0, 6.0, ((0, 16),))
    routes_keys = jax.random.split(jax.random.fold_in(own_keys[2], 1), TOKENS // TOK_DEV)
    routes_turns = jax.random.permutation(jax.random.fold_in(own_keys[2], 3), TOKENS // TOK_DEV)
    routes = jax.vmap(lambda own, number: deal_out(jax.random.fold_in(own_keys[2], 2), own, number, TOK_DEV, EXPERTS, 1, CAP, 2))(routes_keys, routes_turns).reshape((TOKENS, 1))
    gate_fixed = place_ends(jax.random.randint(own_keys[3], (TOKENS,), 4096, 65536), jax.random.fold_in(own_keys[3], 1), 4096, 65535).astype(jnp.int32)
    w_gate = centred(seeds[4], (EXPERTS, FF, D), D ** -0.5, 0.09375, ((0, 4), (1, 4)))
    w_up = centred(seeds[5], (EXPERTS, FF, D), D ** -0.5, 0.09375, ((0, 4), (1, 4)))
    w_down = centred(seeds[6], (EXPERTS, FF, D), FF ** -0.5, 0.21875, ((0, 4), (1, 4)))
    return {"tokens": tokens, "cotangent": cotangent, "routes": routes, "gate_fixed": gate_fixed, "w_gate": w_gate, "w_up": w_up, "w_down": w_down}


def expert_grads(rows_x, rows_g, gate_w, up_w, down_w):
    gate_pre = jnp.dot(rows_x, gate_w.T, preferred_element_type=jnp.float32)
    up_pre = jnp.dot(rows_x, up_w.T, preferred_element_type=jnp.float32)
    sigma_gate = jax.nn.sigmoid(gate_pre)
    hidden = (gate_pre * sigma_gate * up_pre).astype(jnp.bfloat16)
    d_hidden = jnp.dot(rows_g, down_w.T, preferred_element_type=jnp.float32)
    d_gate = (d_hidden * up_pre * sigma_gate * (1.0 + gate_pre * (1.0 - sigma_gate))).astype(jnp.bfloat16)
    d_up = (d_hidden * gate_pre * sigma_gate).astype(jnp.bfloat16)
    grad_down = jnp.dot(hidden.T, rows_g, preferred_element_type=jnp.float32).astype(jnp.bfloat16)
    grad_gate = jnp.dot(d_gate.T, rows_x, preferred_element_type=jnp.float32).astype(jnp.bfloat16)
    grad_up = jnp.dot(d_up.T, rows_x, preferred_element_type=jnp.float32).astype(jnp.bfloat16)
    partial_sum = jnp.dot(d_gate, gate_w, preferred_element_type=jnp.float32) + jnp.dot(d_up, up_w, preferred_element_type=jnp.float32)
    return partial_sum, grad_gate, grad_up, grad_down


def reference(tokens, cotangent, routes, gate_fixed, w_gate, w_up, w_down):
    scaled = ((gate_fixed.astype(jnp.float32) / 65536.0)[:, None] * cotangent.astype(jnp.float32)).astype(jnp.bfloat16)
    expert_of = routes[:, 0]
    most_rows = N_CP * N_TP * CAP

    def per_expert(running, inputs):
        number, gate_w, up_w, down_w = inputs
        chosen = expert_of == number
        positions = jnp.nonzero(chosen, size=most_rows, fill_value=0)[0].astype(jnp.int32)
        filled = (jnp.arange(most_rows) < jnp.sum(chosen.astype(jnp.int32))).astype(jnp.bfloat16)
        rows_x = tokens[positions]
        rows_g = scaled[positions] * filled[:, None]
        partial_sum, grad_gate, grad_up, grad_down = expert_grads(rows_x, rows_g, gate_w, up_w, down_w)
        running = running.at[positions].add(partial_sum)
        return running, (grad_gate, grad_up, grad_down)

    start = jnp.zeros((TOKENS, D), jnp.float32)
    numbers = jnp.arange(EXPERTS).astype(jnp.int32)
    total, (grad_gate, grad_up, grad_down) = lax.scan(per_expert, start, (numbers, w_gate, w_up, w_down))
    return total.astype(jnp.bfloat16), grad_gate, grad_up, grad_down
```

```python
import jax
import jax.numpy as jnp
from jax import lax
from jax.sharding import PartitionSpec as P

BF = jnp.bfloat16
F32 = jnp.float32


def dot(a, b):
    return jnp.dot(a, b, preferred_element_type=F32)


def dot_nt(a, b):
    return lax.dot_general(a, b, (((1,), (1,)), ((), ())), preferred_element_type=F32)


def dot_tn(a, b):
    return lax.dot_general(a, b, (((0,), (0,)), ((), ())), preferred_element_type=F32)


def shards(tokens, cotangent, routes, gate_fixed, w_gate, w_up, w_down):
    n_cp = lax.axis_size("cp")
    n_tp = lax.axis_size("tp")
    local_rows, width = tokens.shape
    cap = local_rows * 3 // 8
    slots = n_cp * cap
    half = slots // 2
    mid = local_rows // 2
    me = lax.axis_index("cp")
    w_gate, w_up, w_down = w_gate[0], w_up[0], w_down[0]

    right = [(i, (i + 1) % n_tp) for i in range(n_tp)]
    left = [(i, (i - 1) % n_tp) for i in range(n_tp)]
    over = [(i, (i + 2) % n_tp) for i in range(n_tp)]

    def go_right(v):
        return lax.ppermute(v, "tp", right)

    def go_left(v):
        return lax.ppermute(v, "tp", left)

    def swap(v, k):
        return lax.ppermute(v, "cp", [(i, i ^ k) for i in range(n_cp)])

    low, high = tokens[:mid], tokens[mid:]
    left_low = go_right(low)
    right_high = go_left(high)
    left_high = go_right(high)
    right_low = go_left(low)
    over_low = go_right(left_low)
    over_high = go_left(right_high)

    relative = jnp.bitwise_xor(routes[:, 0], me)
    same = relative[:, None] == relative[None, :]
    earlier = jnp.arange(local_rows)[None, :] < jnp.arange(local_rows)[:, None]
    ranking = jnp.sum((same & earlier).astype(jnp.int32), axis=1)
    slot = relative * cap + ranking
    slot_left, slot_right = go_right(slot), go_left(slot)
    slot_over = lax.ppermute(slot, "tp", over)

    def placing(slot_of):
        return (slot_of[None, :] == jnp.arange(slots, dtype=jnp.int32)[:, None]).astype(BF)

    def pack(slot_of, rows):
        return dot(placing(slot_of), rows).astype(BF)

    def exchange(packed):
        parts = [packed[k * cap : (k + 1) * cap] for k in range(n_cp)]
        return [parts[0]] + [swap(parts[k], k) for k in range(1, n_cp)]

    scaled = (
        (gate_fixed.astype(F32) / 65536.0)[:, None] * cotangent.astype(F32)
    ).astype(BF)
    got = exchange(pack(slot, scaled))
    g_a = jnp.concatenate(got[:2], axis=0)
    g_b = jnp.concatenate(got[2:], axis=0)
    g_left_a, g_right_a = go_right(g_a), go_left(g_a)
    g_left_b, g_right_b = go_right(g_b), go_left(g_b)
    g_over_a = go_right(g_left_a)
    g_over_b = go_left(g_right_b)
    rows_g = [
        jnp.concatenate(pair, axis=0)
        for pair in (
            (g_a, g_b),
            (g_left_a, g_left_b),
            (g_right_a, g_right_b),
            (g_over_a, g_over_b),
        )
    ]
    rows_x = [
        jnp.concatenate(exchange(pack(slot_of, rows)), axis=0)
        for slot_of, rows in (
            (slot, tokens),
            (slot_left, jnp.concatenate([left_low, left_high], axis=0)),
            (slot_right, jnp.concatenate([right_low, right_high], axis=0)),
            (slot_over, jnp.concatenate([over_low, over_high], axis=0)),
        )
    ]

    hidden, d_gate, d_up, share = [], [], [], []
    for x, g in zip(rows_x, rows_g):
        gate_pre = dot_nt(x, w_gate)
        up_pre = dot_nt(x, w_up)
        d_hidden = dot_nt(g, w_down)
        sigma = jax.nn.sigmoid(gate_pre)
        hidden.append((gate_pre * sigma * up_pre).astype(BF))
        d_gate.append(
            (d_hidden * up_pre * sigma * (1.0 + gate_pre * (1.0 - sigma))).astype(BF)
        )
        d_up.append((d_hidden * gate_pre * sigma).astype(BF))
        share.append(dot(d_gate[-1], w_gate) + dot(d_up[-1], w_up))

    p_left, p_right, p_over = [v.astype(BF) for v in share[1:]]
    direct_b = go_left(p_left[half:])
    direct_a = go_right(p_right[:half])
    via_left = go_left(p_over[:half])
    via_right = go_right(p_over[half:])
    summed_a = go_left((p_left[:half].astype(F32) + via_left.astype(F32)).astype(BF))
    summed_b = go_right((p_right[half:].astype(F32) + via_right.astype(F32)).astype(BF))
    total_a = (share[0][:half] + direct_a.astype(F32) + summed_a.astype(F32)).astype(BF)
    total_b = (share[0][half:] + direct_b.astype(F32) + summed_b.astype(F32)).astype(BF)
    back = jnp.concatenate(
        [total_a[:cap], swap(total_a[cap:], 1), swap(total_b[:cap], 2), swap(total_b[cap:], 3)],
        axis=0,
    )
    grad_tokens = dot_tn(placing(slot), back).astype(BF)

    all_x = jnp.concatenate(rows_x, axis=0)
    all_g = jnp.concatenate(rows_g, axis=0)
    grad_gate = dot_tn(jnp.concatenate(d_gate, axis=0), all_x).astype(BF)
    grad_up = dot_tn(jnp.concatenate(d_up, axis=0), all_x).astype(BF)
    grad_down = dot_tn(jnp.concatenate(hidden, axis=0), all_g).astype(BF)
    return (grad_tokens, grad_gate[None], grad_up[None], grad_down[None])


def solution(mesh):
    rows = P(("dp", "cp", "tp"), None)
    weights = P("cp", "tp", None)
    grads = P(("dp", "cp"), "tp", None)
    return jax.shard_map(
        shards,
        mesh=mesh,
        in_specs=(rows, rows, rows, P(("dp", "cp", "tp")), weights, weights, weights),
        out_specs=(rows, grads, grads, grads),
        check_vma=False,
    )
```

```python
import jax
import jax.numpy as jnp
from jax import lax
from jax.sharding import PartitionSpec as P

BF = jnp.bfloat16
F32 = jnp.float32
DEPTH = 2


def dot(a, b):
    return jnp.dot(a, b, preferred_element_type=F32)


def dot_nt(a, b):
    return lax.dot_general(a, b, (((1,), (1,)), ((), ())), preferred_element_type=F32)


def dot_tn(a, b):
    return lax.dot_general(a, b, (((0,), (0,)), ((), ())), preferred_element_type=F32)


def cat(*parts):
    return jnp.concatenate(parts, axis=0)


class Lane:
    def __init__(self, depth):
        self.depth = depth
        self.sent = []

    def send(self, value, axes, pairs, *waits):
        waits = list(waits)
        if len(self.sent) >= self.depth:
            waits.append(self.sent[-self.depth])
        if waits:
            value = lax.optimization_barrier((value, *waits))[0]
        out = lax.ppermute(value, axes, pairs)
        self.sent.append(out)
        return out


def shards(tokens, cotangent, routes, gate_fixed, w_gate, w_up, w_down):
    n_cp = lax.axis_size("cp")
    n_tp = lax.axis_size("tp")
    local_rows, width = tokens.shape
    cap = local_rows * 3 // 8
    slots = n_cp * cap
    half = slots // 2
    mid = local_rows // 2
    cut = width // 2
    me = lax.axis_index("cp")
    w_gate, w_up, w_down = w_gate[0], w_up[0], w_down[0]

    ring_a, ring_b = [], []
    for c in range(n_cp):
        step = 1 if c % 2 == 0 else -1
        for t in range(n_tp):
            ring_a.append((c * n_tp + t, c * n_tp + (t + step) % n_tp))
            ring_b.append((c * n_tp + t, c * n_tp + (t - step) % n_tp))
    pair_x = [(c, c ^ 2) for c in range(n_cp)]
    pair_core = [(c, c ^ 1) for c in range(n_cp)]
    lane_y, lane_x, lane_c = Lane(DEPTH), Lane(1), Lane(99)

    def send_a(value, *waits):
        return lane_y.send(value, ("cp", "tp"), ring_a, *waits)

    def send_b(value, *waits):
        return lane_y.send(value, ("cp", "tp"), ring_b, *waits)

    def over_x(value, *waits):
        return lane_x.send(value, "cp", pair_x, *waits)

    def over_core(value, *waits):
        return lane_c.send(value, "cp", pair_core, *waits)

    x_first = send_a(tokens)
    x_second = send_b(tokens)

    relative = jnp.bitwise_xor(routes[:, 0], me)
    same = relative[:, None] == relative[None, :]
    earlier = jnp.arange(local_rows)[None, :] < jnp.arange(local_rows)[:, None]
    ranking = jnp.sum((same & earlier).astype(jnp.int32), axis=1)
    slot = relative * cap + ranking
    lane_s = Lane(1)
    slot_of = [
        slot,
        lane_s.send(slot, ("cp", "tp"), ring_a, x_first),
        lane_s.send(slot, ("cp", "tp"), ring_b),
        lane_s.send(slot, "tp", [(t, (t + 2) % n_tp) for t in range(n_tp)]),
    ]

    def placing(which):
        numbers = jnp.arange(slots, dtype=jnp.int32)
        return (slot_of[which][None, :] == numbers[:, None]).astype(BF)

    def pack(which, rows):
        return dot(placing(which), rows).astype(BF)

    scaled = (
        (gate_fixed.astype(F32) / 65536.0)[:, None] * cotangent.astype(F32)
    ).astype(BF)
    packed_g = pack(0, scaled)
    g_x = over_x(packed_g[half:])
    g_1 = over_core(packed_g[cap:half])
    g_a = cat(packed_g[:cap], g_1)
    g_first_a = send_a(g_a)
    g_3 = over_core(g_x[cap:])
    g_b = cat(g_x[:cap], g_3)

    def exchange_x(which, rows):
        packed = pack(which, rows)
        via_x = over_x(packed[half:])
        return cat(packed[:cap], via_x[:cap]), cat(packed[cap:half], via_x[cap:])

    def exchange_core(kept, passed):
        got = over_core(passed)
        return cat(kept[:cap], got[:cap], kept[cap:], got[cap:])

    g_second_b = send_b(g_b)
    kept_1, passed_1 = exchange_x(1, x_first)
    x_over_a = send_a(x_first[:mid])
    x_over_b = send_b(x_second[mid:])
    kept_2, passed_2 = exchange_x(2, x_second)
    x_rows_1 = exchange_core(kept_1, passed_2)
    x_rows_2 = exchange_core(kept_2, passed_1)
    g_first_b = send_a(g_b)
    g_second_a = send_b(g_a)
    x_rows_3 = exchange_core(*exchange_x(3, cat(x_over_a, x_over_b)))
    g_over_a = send_a(g_first_a)
    g_over_b = send_b(g_second_b)

    def block(x, g):
        gate_pre = dot_nt(x, w_gate)
        up_pre = dot_nt(x, w_up)
        d_hidden = dot_nt(g, w_down)
        sigma = jax.nn.sigmoid(gate_pre)
        hidden = (gate_pre * sigma * up_pre).astype(BF)
        d_gate = (d_hidden * up_pre * sigma * (1.0 + gate_pre * (1.0 - sigma))).astype(BF)
        d_up = (d_hidden * gate_pre * sigma).astype(BF)
        share = (dot(d_gate, w_gate) + dot(d_up, w_up)).astype(BF)
        return (x, g, hidden, d_gate, d_up), share[:, :cut], share[:, cut:]

    def to_core(share):
        return over_core(cat(share[cap:half], share[half + cap :]))

    def to_tokens(which, share, crossed):
        got = over_x(cat(share[half : half + cap], crossed[cap:]))
        rows = cat(share[:cap], crossed[:cap], got)
        return dot_tn(placing(which), rows).astype(BF)

    def add(*parts):
        total = parts[0].astype(F32)
        for part in parts[1:]:
            total = total + part.astype(F32)
        return total.astype(BF)

    done_1, p_1, q_1 = block(x_rows_1, cat(g_first_a, g_first_b))
    done_2, p_2, q_2 = block(x_rows_2, cat(g_second_a, g_second_b))
    crossed_2 = to_core(q_1)
    crossed_1 = to_core(q_2)
    q_1 = to_tokens(1, q_1, crossed_1)
    x_rows_0 = exchange_core(*exchange_x(0, tokens))
    direct_b = send_b(p_1[half:])
    direct_a = send_a(p_2[:half])
    done_3, p_3, q_3 = block(x_rows_3, cat(g_over_a, g_over_b))
    via_b = send_b(p_3[:half])
    via_a = send_a(p_3[half:])
    q_3 = to_tokens(3, q_3, to_core(q_3))
    done_0, p_0, q_0 = block(x_rows_0, cat(g_a, g_b))
    summed_b = send_b(add(p_1[:half], via_b))
    summed_a = send_a(add(p_2[half:], via_a))
    q_via_b = send_b(q_3[:mid])
    q_via_a = send_a(q_3[mid:])
    q_2 = to_tokens(2, q_2, crossed_2)
    q_from_second = send_b(cat(add(q_1[:mid], q_via_b), q_1[mid:]))
    q_from_first = send_a(cat(q_2[:mid], add(q_2[mid:], q_via_a)))
    q_0 = to_tokens(0, q_0, to_core(q_0))
    total = cat(add(p_0[:half], direct_a, summed_b), add(p_0[half:], direct_b, summed_a))
    grad_tokens = jnp.concatenate(
        [to_tokens(0, total, to_core(total)), add(q_0, q_from_first, q_from_second)], axis=1
    )

    rows_x, rows_g, hidden, d_gate, d_up = zip(done_1, done_2, done_3, done_0)
    all_x = cat(*rows_x)
    all_g = cat(*rows_g)
    grad_gate = dot_tn(cat(*d_gate), all_x).astype(BF)
    grad_up = dot_tn(cat(*d_up), all_x).astype(BF)
    grad_down = dot_tn(cat(*hidden), all_g).astype(BF)
    return (grad_tokens, grad_gate[None], grad_up[None], grad_down[None])


def solution(mesh):
    rows = P(("dp", "cp", "tp"), None)
    weights = P("cp", "tp", None)
    grads = P(("dp", "cp"), "tp", None)
    return jax.shard_map(
        shards,
        mesh=mesh,
        in_specs=(rows, rows, rows, P(("dp", "cp", "tp")), weights, weights, weights),
        out_specs=(rows, grads, grads, grads),
        check_vma=False,
    )
```

```python
import jax
import jax.numpy as jnp
from jax import lax
from jax.sharding import PartitionSpec as P

BF = jnp.bfloat16
F32 = jnp.float32
DEPTH = 3
DEPTH_BACK = 4
PIECES = 2


def dot(a, b):
    return jnp.dot(a, b, preferred_element_type=F32)


def dot_nt(a, b):
    return lax.dot_general(a, b, (((1,), (1,)), ((), ())), preferred_element_type=F32)


def dot_tn(a, b):
    return lax.dot_general(a, b, (((0,), (0,)), ((), ())), preferred_element_type=F32)


def cat(*parts):
    return jnp.concatenate(parts, axis=0)


class Lane:
    def __init__(self, depth):
        self.depth = depth
        self.sent = []

    def send(self, value, axes, pairs, *waits):
        waits = list(waits)
        if len(self.sent) >= self.depth:
            waits.append(self.sent[-self.depth])
        if waits:
            value = lax.optimization_barrier((value, *waits))[0]
        out = lax.ppermute(value, axes, pairs)
        self.sent.append(out)
        return out


def shards(tokens, cotangent, routes, gate_fixed, w_gate, w_up, w_down):
    n_cp = lax.axis_size("cp")
    n_tp = lax.axis_size("tp")
    local_rows, width = tokens.shape
    cap = local_rows * 3 // 8
    slots = n_cp * cap
    half = slots // 2
    mid = local_rows // 2
    me = lax.axis_index("cp")
    w_gate, w_up, w_down = w_gate[0], w_up[0], w_down[0]

    ring_a, ring_b = [], []
    for c in range(n_cp):
        step = 1 if c % 2 == 0 else -1
        for t in range(n_tp):
            ring_a.append((c * n_tp + t, c * n_tp + (t + step) % n_tp))
            ring_b.append((c * n_tp + t, c * n_tp + (t - step) % n_tp))
    pair_x = [(c, c ^ 2) for c in range(n_cp)]
    pair_core = [(c, c ^ 1) for c in range(n_cp)]
    lane_y, lane_x, lane_c = Lane(DEPTH), Lane(1), Lane(99)

    def send_a(value, *waits):
        return lane_y.send(value, ("cp", "tp"), ring_a, *waits)

    def send_b(value, *waits):
        return lane_y.send(value, ("cp", "tp"), ring_b, *waits)

    def over_x(value, *waits):
        return lane_x.send(value, "cp", pair_x, *waits)

    def over_core(value, *waits):
        return lane_c.send(value, "cp", pair_core, *waits)

    relative = jnp.bitwise_xor(routes[:, 0], me)
    same = relative[:, None] == relative[None, :]
    earlier = jnp.arange(local_rows)[None, :] < jnp.arange(local_rows)[:, None]
    ranking = jnp.sum((same & earlier).astype(jnp.int32), axis=1)
    slot = relative * cap + ranking
    beside = jnp.broadcast_to(slot.astype(BF)[:, None], (local_rows, 128))
    x_own = jnp.concatenate([tokens, beside], axis=1)
    x_first = send_a(x_own)
    x_second = send_b(x_own)

    numbers = jnp.arange(slots, dtype=jnp.int32)
    placing_own = (slot[:, None] == numbers[None, :]).astype(BF)

    def pack_own(rows):
        return dot_tn(placing_own, rows).astype(BF)

    def pack(rows):
        slot_of = rows[:, width:].astype(jnp.int32)
        placing = (slot_of[:, :1] == numbers[None, :]).astype(BF)
        return dot_tn(placing, rows[:, :width]).astype(BF)

    scaled = (
        (gate_fixed.astype(F32) / 65536.0)[:, None] * cotangent.astype(F32)
    ).astype(BF)
    def exchange_x(packed):
        via_x = over_x(packed[half:])
        return cat(packed[:cap], via_x[:cap]), cat(packed[cap:half], via_x[cap:])

    def exchange_core(kept, passed):
        got = over_core(passed)
        return cat(kept[:cap], got[:cap], kept[cap:], got[cap:])

    g_own = exchange_core(*exchange_x(pack_own(scaled)))
    kept_1, passed_1 = exchange_x(pack(x_first))
    x_over_a = send_a(x_first[:mid])
    x_over_b = send_b(x_second[mid:])
    g_first = send_a(g_own)
    g_second = send_b(g_own)
    kept_2, passed_2 = exchange_x(pack(x_second))
    x_rows_1 = exchange_core(kept_1, passed_2)
    x_rows_2 = exchange_core(kept_2, passed_1)
    x_rows_3 = exchange_core(*exchange_x(pack(cat(x_over_a, x_over_b))))
    g_over_a = send_a(g_first[:half])
    g_over_b = send_b(g_second[half:])

    def block(x, g):
        gate_pre = dot_nt(x, w_gate)
        up_pre = dot_nt(x, w_up)
        d_hidden = dot_nt(g, w_down)
        sigma = jax.nn.sigmoid(gate_pre)
        hidden = (gate_pre * sigma * up_pre).astype(BF)
        d_gate = (d_hidden * up_pre * sigma * (1.0 + gate_pre * (1.0 - sigma))).astype(BF)
        d_up = (d_hidden * gate_pre * sigma).astype(BF)
        return (x, g, hidden, d_gate, d_up), dot(d_gate, w_gate) + dot(d_up, w_up)

    def add(*parts):
        total = parts[0].astype(F32)
        for part in parts[1:]:
            total = total + part.astype(F32)
        return total.astype(BF)

    lane_y.depth = DEPTH_BACK
    done_1, p_1 = block(x_rows_1, g_first)
    done_2, p_2 = block(x_rows_2, g_second)
    p_1, p_2 = p_1.astype(BF), p_2.astype(BF)
    direct_b = send_b(p_1[half:])
    direct_a = send_a(p_2[:half])
    done_0, p_0 = block(exchange_core(*exchange_x(pack_own(tokens))), g_own)
    done_3, p_3 = block(x_rows_3, cat(g_over_a, g_over_b))
    p_3 = p_3.astype(BF)
    via_b = send_b(p_3[:half])
    via_a = send_a(p_3[half:])
    pieces = [slice(i * width // PIECES, (i + 1) * width // PIECES) for i in range(PIECES)]
    kept = [
        lax.optimization_barrier(tuple(v[:, s] for v in (p_0, p_1, p_2, direct_a, direct_b, via_a, via_b)))
        for s in pieces
    ]
    summed = [
        (send_b(add(first[:half], v_b)), send_a(add(second[half:], v_a)))
        for _, first, second, _, _, v_a, v_b in kept
    ]
    grads = []
    for (own, _, _, d_a, d_b, _, _), (summed_b, summed_a) in zip(kept, summed):
        low = add(own[:half], d_a, summed_b)
        high = add(own[half:], d_b, summed_a)
        crossed = over_core(cat(low[cap:], high[cap:]))
        got = over_x(cat(high[:cap], crossed[cap:]))
        grads.append(dot(placing_own, cat(low[:cap], crossed[:cap], got)).astype(BF))
    grad_tokens = jnp.concatenate(grads, axis=1)

    rows_x, rows_g, hidden, d_gate, d_up = zip(done_1, done_2, done_3, done_0)
    all_x = cat(*rows_x)
    all_g = cat(*rows_g)
    grad_gate = dot_tn(cat(*d_gate), all_x).astype(BF)
    grad_up = dot_tn(cat(*d_up), all_x).astype(BF)
    grad_down = dot_tn(cat(*hidden), all_g).astype(BF)
    return (grad_tokens, grad_gate[None], grad_up[None], grad_down[None])


def solution(mesh):
    rows = P(("dp", "cp", "tp"), None)
    weights = P("cp", "tp", None)
    grads = P(("dp", "cp"), "tp", None)
    return jax.shard_map(
        shards,
        mesh=mesh,
        in_specs=(rows, rows, rows, P(("dp", "cp", "tp")), weights, weights, weights),
        out_specs=(rows, grads, grads, grads),
        check_vma=False,
    )
```

```python
import jax
import jax.numpy as jnp
from jax import lax
from jax.sharding import PartitionSpec as P

BF = jnp.bfloat16
F32 = jnp.float32
DEPTH = 2
DEPTH_BACK = 3
DEPTH_LAST = 2
PIECES = 2


def dot(a, b):
    return jnp.dot(a, b, preferred_element_type=F32)


def dot_nt(a, b):
    return lax.dot_general(a, b, (((1,), (1,)), ((), ())), preferred_element_type=F32)


def dot_tn(a, b):
    return lax.dot_general(a, b, (((0,), (0,)), ((), ())), preferred_element_type=F32)


def cat(*parts):
    return jnp.concatenate(parts, axis=0)


class Lane:
    def __init__(self, depth):
        self.depth = depth
        self.sent = []

    def send(self, value, axes, pairs, *waits):
        waits = list(waits)
        if len(self.sent) >= self.depth:
            waits.append(self.sent[-self.depth])
        if waits:
            value = lax.optimization_barrier((value, *waits))[0]
        out = lax.ppermute(value, axes, pairs)
        self.sent.append(out)
        return out


def shards(tokens, cotangent, routes, gate_fixed, w_gate, w_up, w_down):
    n_cp = lax.axis_size("cp")
    n_tp = lax.axis_size("tp")
    local_rows, width = tokens.shape
    cap = local_rows * 3 // 8
    slots = n_cp * cap
    half = slots // 2
    mid = local_rows // 2
    me = lax.axis_index("cp")
    w_gate, w_up, w_down = w_gate[0], w_up[0], w_down[0]

    ring_a, ring_b = [], []
    for c in range(n_cp):
        step = 1 if c % 2 == 0 else -1
        for t in range(n_tp):
            ring_a.append((c * n_tp + t, c * n_tp + (t + step) % n_tp))
            ring_b.append((c * n_tp + t, c * n_tp + (t - step) % n_tp))
    pair_x = [(c, c ^ 2) for c in range(n_cp)]
    pair_core = [(c, c ^ 1) for c in range(n_cp)]
    lane_y, lane_x, lane_c = Lane(DEPTH), Lane(1), Lane(99)

    def send_a(value, *waits):
        return lane_y.send(value, ("cp", "tp"), ring_a, *waits)

    def send_b(value, *waits):
        return lane_y.send(value, ("cp", "tp"), ring_b, *waits)

    def over_x(value, *waits):
        return lane_x.send(value, "cp", pair_x, *waits)

    def over_core(value, *waits):
        return lane_c.send(value, "cp", pair_core, *waits)

    relative = jnp.bitwise_xor(routes[:, 0], me)
    same = relative[:, None] == relative[None, :]
    earlier = jnp.arange(local_rows)[None, :] < jnp.arange(local_rows)[:, None]
    ranking = jnp.sum((same & earlier).astype(jnp.int32), axis=1)
    slot = relative * cap + ranking
    beside = jnp.broadcast_to(slot.astype(BF)[:, None], (local_rows, 128))
    x_own = jnp.concatenate([tokens, beside], axis=1)
    x_first = send_a(x_own)
    x_second = send_b(x_own)

    numbers = jnp.arange(slots, dtype=jnp.int32)
    placing_own = (slot[:, None] == numbers[None, :]).astype(BF)

    def pack_own(rows):
        return dot_tn(placing_own, rows).astype(BF)

    def pack(rows):
        slot_of = rows[:, width:].astype(jnp.int32)
        placing = (slot_of[:, :1] == numbers[None, :]).astype(BF)
        return dot_tn(placing, rows[:, :width]).astype(BF)

    def exchange(packed, *waits):
        got = over_x(packed[half:], *waits)
        return cat(packed[:cap], got[:cap], packed[cap:half], got[cap:])

    scaled = (
        (gate_fixed.astype(F32) / 65536.0)[:, None] * cotangent.astype(F32)
    ).astype(BF)
    g_own = exchange(pack_own(scaled))
    theirs = [over_core(w) for w in (w_gate, w_up, w_down)]
    weights = [(w_gate, w_up, w_down), theirs]
    x_over_a = send_a(x_first[:mid])
    x_over_b = send_b(x_second[mid:])
    rows_1 = exchange(pack(x_first), *theirs[:2])
    g_first = send_a(g_own)
    g_second = send_b(g_own)
    rows_2 = exchange(pack(x_second), theirs[2])
    rows_3 = exchange(pack(cat(x_over_a, x_over_b)))
    rows_0 = exchange(pack_own(tokens))
    g_over_a = send_a(g_first[:half])
    g_over_b = send_b(g_second[half:])

    def side_of(x, g, gate_w, up_w, down_w):
        gate_pre = dot_nt(x, gate_w)
        up_pre = dot_nt(x, up_w)
        d_hidden = dot_nt(g, down_w)
        sigma = jax.nn.sigmoid(gate_pre)
        hidden = (gate_pre * sigma * up_pre).astype(BF)
        d_gate = (d_hidden * up_pre * sigma * (1.0 + gate_pre * (1.0 - sigma))).astype(BF)
        d_up = (d_hidden * gate_pre * sigma).astype(BF)
        share = dot(d_gate, gate_w) + dot(d_up, up_w)
        return (x, g, hidden, d_gate, d_up), share.astype(BF)

    def block(x, g):
        sides = [
            side_of(x[i * half : (i + 1) * half], g[i * half : (i + 1) * half], *weights[i])
            for i in range(2)
        ]
        return tuple(zip(sides[0][0], sides[1][0])), [side[1] for side in sides]

    def add(*parts):
        total = parts[0].astype(F32)
        for part in parts[1:]:
            total = total + part.astype(F32)
        return total.astype(BF)

    lane_y.depth = DEPTH_BACK
    done_1, p_1 = block(rows_1, g_first)
    done_2, p_2 = block(rows_2, g_second)
    direct_b = send_b(p_1[1])
    direct_a = send_a(p_2[0])
    done_3, p_3 = block(rows_3, cat(g_over_a, g_over_b))
    done_0, p_0 = block(rows_0, g_own)
    via_b = send_b(p_3[0])
    via_a = send_a(p_3[1])
    pieces = [slice(i * width // PIECES, (i + 1) * width // PIECES) for i in range(PIECES)]
    kept = [
        lax.optimization_barrier(tuple(v[:, s] for v in (*p_0, p_1[0], p_2[1], direct_a, direct_b, via_a, via_b)))
        for s in pieces
    ]
    lane_y.depth = DEPTH_LAST
    summed = [
        (send_b(add(first, v_b)), send_a(add(second, v_a)))
        for _, _, first, second, _, _, v_a, v_b in kept
    ]
    grads = []
    for (own_0, own_1, _, _, d_a, d_b, _, _), (summed_b, summed_a) in zip(kept, summed):
        low = add(own_0, d_a, summed_b)
        high = add(own_1, d_b, summed_a)
        got = over_x(cat(low[cap:], high[cap:]))
        grads.append(dot(placing_own, cat(low[:cap], high[:cap], got)).astype(BF))
    grad_tokens = jnp.concatenate(grads, axis=1)

    x, g, hidden, d_gate, d_up = [
        [cat(*(v[side] for v in parts)) for side in range(2)]
        for parts in zip(done_1, done_2, done_3, done_0)
    ]

    def weight_grad(left, right):
        theirs = over_core(dot_tn(left[1], right[1]).astype(BF))
        return (dot_tn(left[0], right[0]) + theirs.astype(F32)).astype(BF)[None]

    grad_gate = weight_grad(d_gate, x)
    grad_up = weight_grad(d_up, x)
    grad_down = weight_grad(hidden, g)
    return (grad_tokens, grad_gate, grad_up, grad_down)


def solution(mesh):
    rows = P(("dp", "cp", "tp"), None)
    weights = P("cp", "tp", None)
    grads = P(("dp", "cp"), "tp", None)
    return jax.shard_map(
        shards,
        mesh=mesh,
        in_specs=(rows, rows, rows, P(("dp", "cp", "tp")), weights, weights, weights),
        out_specs=(rows, grads, grads, grads),
        check_vma=False,
    )
```

```python
import jax
import jax.numpy as jnp
from jax import lax
from jax.sharding import PartitionSpec as P

BF = jnp.bfloat16
F32 = jnp.float32
DEPTH = 2
DEPTH_BACK = 3
DEPTH_LAST = 3
PIECES = 1


def dot(a, b):
    return jnp.dot(a, b, preferred_element_type=F32)


def dot_nt(a, b):
    return lax.dot_general(a, b, (((1,), (1,)), ((), ())), preferred_element_type=F32)


def dot_tn(a, b):
    return lax.dot_general(a, b, (((0,), (0,)), ((), ())), preferred_element_type=F32)


def cat(*parts):
    return jnp.concatenate(parts, axis=0)


class Lane:
    def __init__(self, depth):
        self.depth = depth
        self.sent = []

    def send(self, value, axes, pairs, *waits):
        waits = list(waits)
        if len(self.sent) >= self.depth:
            waits.append(self.sent[-self.depth])
        if waits:
            value = lax.optimization_barrier((value, *waits))[0]
        out = lax.ppermute(value, axes, pairs)
        self.sent.append(out)
        return out


def shards(tokens, cotangent, routes, gate_fixed, w_gate, w_up, w_down):
    n_cp = lax.axis_size("cp")
    n_tp = lax.axis_size("tp")
    local_rows, width = tokens.shape
    cap = local_rows * 3 // 8
    slots = n_cp * cap
    half = slots // 2
    mid = local_rows // 2
    me = lax.axis_index("cp")
    w_gate, w_up, w_down = w_gate[0], w_up[0], w_down[0]

    ring_a, ring_b = [], []
    for c in range(n_cp):
        step = 1 if c % 2 == 0 else -1
        for t in range(n_tp):
            ring_a.append((c * n_tp + t, c * n_tp + (t + step) % n_tp))
            ring_b.append((c * n_tp + t, c * n_tp + (t - step) % n_tp))
    pair_x = [(c, c ^ 2) for c in range(n_cp)]
    pair_core = [(c, c ^ 1) for c in range(n_cp)]
    lane_y, lane_x, lane_c = Lane(DEPTH), Lane(1), Lane(99)

    def send_a(value, *waits):
        return lane_y.send(value, ("cp", "tp"), ring_a, *waits)

    def send_b(value, *waits):
        return lane_y.send(value, ("cp", "tp"), ring_b, *waits)

    def over_x(value, *waits):
        return lane_x.send(value, "cp", pair_x, *waits)

    def over_core(value, *waits):
        return lane_c.send(value, "cp", pair_core, *waits)

    relative = jnp.bitwise_xor(routes[:, 0], me)
    same = relative[:, None] == relative[None, :]
    earlier = jnp.arange(local_rows)[None, :] < jnp.arange(local_rows)[:, None]
    ranking = jnp.sum((same & earlier).astype(jnp.int32), axis=1)
    slot = relative * cap + ranking
    beside = jnp.broadcast_to(slot.astype(BF)[:, None], (local_rows, 128))
    x_own = jnp.concatenate([tokens, beside], axis=1)
    x_first = send_a(x_own)
    x_second = send_b(x_own)

    numbers = jnp.arange(slots, dtype=jnp.int32)
    placing_own = (slot[:, None] == numbers[None, :]).astype(BF)

    def pack_own(rows):
        return dot_tn(placing_own, rows).astype(BF)

    def pack(rows):
        slot_of = rows[:, width:].astype(jnp.int32)
        placing = (slot_of[:, :1] == numbers[None, :]).astype(BF)
        return dot_tn(placing, rows[:, :width]).astype(BF)

    def exchange(packed, *waits):
        got = over_x(packed[half:], *waits)
        return cat(packed[:cap], got[:cap], packed[cap:half], got[cap:])

    scaled = (
        (gate_fixed.astype(F32) / 65536.0)[:, None] * cotangent.astype(F32)
    ).astype(BF)
    g_own = exchange(pack_own(scaled))
    theirs = [over_core(w) for w in (w_gate, w_up, w_down)]
    weights = [(w_gate, w_up, w_down), theirs]
    x_over_a = send_a(x_first[:mid])
    x_over_b = send_b(x_second[mid:])
    rows_1 = exchange(pack(x_first), *theirs[:2])
    g_first = send_a(g_own)
    g_second = send_b(g_own)
    rows_2 = exchange(pack(x_second), theirs[2])
    rows_3 = exchange(pack(cat(x_over_a, x_over_b)))
    rows_0 = exchange(pack_own(tokens))
    g_over_a = send_a(g_first[:half])
    g_over_b = send_b(g_second[half:])

    def side_of(x, g, gate_w, up_w, down_w):
        gate_pre = dot_nt(x, gate_w)
        up_pre = dot_nt(x, up_w)
        d_hidden = dot_nt(g, down_w)
        sigma = jax.nn.sigmoid(gate_pre)
        hidden = (gate_pre * sigma * up_pre).astype(BF)
        d_gate = (d_hidden * up_pre * sigma * (1.0 + gate_pre * (1.0 - sigma))).astype(BF)
        d_up = (d_hidden * gate_pre * sigma).astype(BF)
        share = dot(d_gate, gate_w) + dot(d_up, up_w)
        return (x, g, hidden, d_gate, d_up), share.astype(BF)

    def block(x, g):
        sides = [
            side_of(x[i * half : (i + 1) * half], g[i * half : (i + 1) * half], *weights[i])
            for i in range(2)
        ]
        return tuple(zip(sides[0][0], sides[1][0])), [side[1] for side in sides]

    def add(*parts):
        total = parts[0].astype(F32)
        for part in parts[1:]:
            total = total + part.astype(F32)
        return total.astype(BF)

    lane_y.depth = DEPTH_BACK
    done_1, p_1 = block(rows_1, g_first)
    done_2, p_2 = block(rows_2, g_second)
    direct_b = send_b(p_1[1])
    direct_a = send_a(p_2[0])
    done_3, p_3 = block(rows_3, cat(g_over_a, g_over_b))
    done_0, p_0 = block(rows_0, g_own)
    via_b = send_b(p_3[0])
    via_a = send_a(p_3[1])
    pieces = [slice(i * width // PIECES, (i + 1) * width // PIECES) for i in range(PIECES)]
    kept = [
        lax.optimization_barrier(tuple(v[:, s] for v in (*p_0, p_1[0], p_2[1], direct_a, direct_b, via_a, via_b)))
        for s in pieces
    ]
    lane_y.depth = DEPTH_LAST
    summed = [
        (send_b(add(first, v_b)), send_a(add(second, v_a)))
        for _, _, first, second, _, _, v_a, v_b in kept
    ]
    grads = []
    for (own_0, own_1, _, _, d_a, d_b, _, _), (summed_b, summed_a) in zip(kept, summed):
        low = add(own_0, d_a, summed_b)
        high = add(own_1, d_b, summed_a)
        got = over_x(cat(low[cap:], high[cap:]))
        grads.append(dot(placing_own, cat(low[:cap], high[:cap], got)).astype(BF))
    grad_tokens = jnp.concatenate(grads, axis=1)

    x, g, hidden, d_gate, d_up = [
        [cat(*(v[side] for v in parts)) for side in range(2)]
        for parts in zip(done_1, done_2, done_3, done_0)
    ]

    def weight_grad(left, right):
        theirs = over_core(dot_tn(left[1], right[1]).astype(BF))
        return (dot_tn(left[0], right[0]) + theirs.astype(F32)).astype(BF)[None]

    grad_gate = weight_grad(d_gate, x)
    grad_up = weight_grad(d_up, x)
    grad_down = weight_grad(hidden, g)
    return (grad_tokens, grad_gate, grad_up, grad_down)


def solution(mesh):
    rows = P(("dp", "cp", "tp"), None)
    weights = P("cp", "tp", None)
    grads = P(("dp", "cp"), "tp", None)
    return jax.shard_map(
        shards,
        mesh=mesh,
        in_specs=(rows, rows, rows, P(("dp", "cp", "tp")), weights, weights, weights),
        out_specs=(rows, grads, grads, grads),
        check_vma=False,
    )
```
